32 devices in a mesh: tm: 2 (over y), space: 16 (over z, x, core).
Axes of the slice: x: 2, y: 2, z: 4, core: 2. Of those that a mesh axis runs over, the one named last changes fastest.
Arguments:
- fine_nodes: float32 [2, 3, 128, 128, 256], P('tm', None, 'space'), may hold values from -1.25 to 1.25
- fine_implicit: float32 [2, 3, 128, 128, 256], P('tm', None, 'space'), may hold values from -18 to 18
Outputs:
- new_nodes: float32 [2, 3, 128, 128, 256], P('tm', None, 'space')
- new_implicit: float32 [2, 2, 128, 128, 256], P('tm', None, 'space')
The draws below stay inside these ranges and needn't reach their ends.
All inputs are finite; a program needn't handle non-finite values.
Results may differ from the reference program's by a relative error of at most 0.00014.
Values sent between devices are 32-bit elements; how exact they have to be, the bound alone decides.
A program may use at most 128 MiB of HBM per device.

```python
import math
import jax
import jax.numpy as jnp

NX = 128
NY = 128
NZ = 256
NODES = 3
SLICES = 2


def draw_fine_nodes(key, part):
    key_sign = jax.random.fold_in(key, 11)
    key_field = jax.random.fold_in(key, 12)
    bits = jax.random.randint(key_sign, (SLICES, 1, NX // 2, 1, 1, 1), 0, 2)
    signs = (2 * bits - 1).astype(jnp.float32)
    signs = jnp.broadcast_to(signs, (SLICES, NODES, NX // 2, 2, NY, NZ)).reshape(SLICES, NODES, NX, NY, NZ)
    field = jax.random.uniform(key_field, (SLICES, NODES, NX, NY, NZ), jnp.float32, -1.0, 1.0)
    return 1.1 * signs + 0.1 * field


def steps_of(stream_key, shape, pieces, low, high):
    level = 1.0
    for dim, parts in pieces:
        steps = jax.random.uniform(jax.random.fold_in(jax.random.fold_in(stream_key, 6), dim), (parts,), jnp.float32, low / len(pieces), high / len(pieces))
        level = level * jnp.repeat(jnp.exp(steps), shape[dim] // parts).reshape((-1,) + (1,) * (len(shape) - 1 - dim))
    return level


def noise(key, dims, scale, bound, pieces=(), kind=jnp.bfloat16):
    entries = jax.random.normal(key, dims, jnp.float32) * scale
    if len(pieces) > 0:
        entries = steps_of(key, dims, pieces, -0.22, 0.18) * entries
    return jnp.clip(entries, min=-bound, max=bound).astype(kind)


def setup_inputs(seed: int = 0) -> dict:
    key_list = jax.random.split(jax.random.key(seed), 3)
    fine_nodes = draw_fine_nodes(jax.random.fold_in(key_list[2], 71), 0)
    fine_implicit = noise(key_list[1], (SLICES, NODES, NX, NY, NZ), 3.0, 18.0, ((0, 2), (2, 16)), jnp.float32)
    return {"fine_nodes": fine_nodes, "fine_implicit": fine_implicit}


WEIGHTS = ((5.0 / 24.0, 1.0 / 3.0, -1.0 / 24.0), (-1.0 / 24.0, 1.0 / 3.0, 5.0 / 24.0))
EPS2 = 2.0


def react(u):
    return u - u * u * u


def restrict(stacked):
    k, a, b, c = stacked.shape
    return stacked.reshape(k, a // 2, 2, b // 2, 2, c // 2, 2).mean(axis=(2, 4, 6))


def coarse_rate(stacked):
    lap = jnp.roll(stacked, -1, 1) + jnp.roll(stacked, 1, 1)
    lap = lap + jnp.roll(stacked, -1, 2) + jnp.roll(stacked, 1, 2)
    lap = lap + jnp.roll(stacked, -1, 3) + jnp.roll(stacked, 1, 3)
    return EPS2 * ((lap - 6.0 * stacked) * 0.25) + react(stacked)


def spread(values, following, axis):
    middle = 0.5 * (values + following)
    both = jnp.stack([values, middle], axis=axis + 1)
    shape = list(values.shape)
    shape[axis] = shape[axis] * 2
    return both.reshape(shape)


def refine(stacked):
    out = spread(stacked, jnp.roll(stacked, -1, 1), 1)
    out = spread(out, jnp.roll(out, -1, 2), 2)
    return spread(out, jnp.roll(out, -1, 3), 3)


def wave_square(size):
    kappa = (2.0 * math.pi) * jnp.fft.fftfreq(size).astype(jnp.float32)
    return kappa * kappa


def coarse_sweep(start, rates, sums):
    first = start + 0.25 * (coarse_rate(start[None])[0] - rates[0]) + sums[0]
    second = first + 0.25 * (coarse_rate(first[None])[0] - rates[1]) + sums[1]
    return first, second


def reference(fine_nodes, fine_implicit):
    lam = wave_square(NX)[:, None, None] + wave_square(NY)[None, :, None] + wave_square(NZ)[None, None, :]
    factor = 1.0 / (1.0 + 0.5 * lam)
    node_list = []
    term_list = []
    previous_end = None
    for slot in range(SLICES):
        nodes = fine_nodes[slot]
        implicit = fine_implicit[slot]
        explicit_old = react(nodes)
        rates_old = explicit_old + implicit
        values = [nodes[0]]
        terms = [implicit[0]]
        for m in range(2):
            w = WEIGHTS[m]
            quad = 0.5 * (w[0] * rates_old[0] + w[1] * rates_old[1] + w[2] * rates_old[2])
            rhs = values[m] + 0.25 * (react(values[m]) - explicit_old[m]) - 0.25 * implicit[m + 1] + quad
            solved = jnp.real(jnp.fft.ifftn(jnp.fft.fftn(rhs) * factor)).astype(rhs.dtype)
            values.append(solved)
            terms.append((solved - rhs) * 4.0)
        fresh = jnp.stack(values)
        rates_new = react(fresh) + jnp.stack(terms)
        sums = restrict(jnp.stack([0.5 * (w[0] * rates_new[0] + w[1] * rates_new[1] + w[2] * rates_new[2]) for w in WEIGHTS]))
        coarse = restrict(fresh)
        rates_c = coarse_rate(coarse[:2])
        start = coarse[0] if slot == 0 else previous_end
        first, second = coarse_sweep(start, rates_c, sums)
        previous_end_new = second
        delta = jnp.stack([first - coarse[1], second - coarse[2]])
        corr = refine(delta)
        fixed_one = values[1] + corr[0]
        fixed_two = values[2] + corr[1]
        if slot == 0:
            head = nodes[0]
        else:
            head = node_list[slot - 1][2]
        node_list.append(jnp.stack([head, fixed_one, fixed_two]))
        term_list.append(jnp.stack([terms[1], terms[2]]))
        previous_end = previous_end_new
    return jnp.stack(node_list), jnp.stack(term_list)
```

```python
import math

import jax
import jax.numpy as jnp
from jax import lax
from jax.sharding import PartitionSpec as P

WEIGHTS = ((5.0 / 24.0, 1.0 / 3.0, -1.0 / 24.0), (-1.0 / 24.0, 1.0 / 3.0, 5.0 / 24.0))
EPS2 = 2.0
HIGHEST = lax.Precision.HIGHEST


def extended(block, sides, width):
    for axis, dim in sides:
        count = lax.axis_size(axis)
        forward = [(i, i + 1) for i in range(count - 1)]
        forward.append((count - 1, 0))
        backward = [(target, source) for source, target in forward]
        low = lax.ppermute(
            lax.slice_in_dim(block, block.shape[dim] - width, None, axis=dim), axis, forward
        )
        high = lax.ppermute(lax.slice_in_dim(block, 0, width, axis=dim), axis, backward)
        block = jnp.concatenate([low, block, high], axis=dim)
    return block


def passed_along(value, axis, steps):
    count = lax.axis_size(axis)
    leading, last = (max(0, -steps), min(count, count - steps))
    return lax.ppermute(value, axis, [(source, source + steps) for source in range(leading, last)])


def shifted(value, axis, steps):
    count = lax.axis_size(axis)
    pairs = [(source, (source + steps) % count) for source in range(count)]
    return lax.ppermute(value, axis, pairs)


def react(u):
    return u - u * u * u


def real_basis(size):
    rows = lax.broadcasted_iota(jnp.int32, (size, size), 0)
    cells = lax.broadcasted_iota(jnp.int32, (size, size), 1)
    half = size // 2
    freq = jnp.where(rows <= half, rows, rows - half)
    phase = (freq * cells % size).astype(jnp.float32) * (2.0 * math.pi / size)
    scale = jnp.where((rows == 0) | (rows == half), 1.0 / math.sqrt(size), math.sqrt(2.0 / size))
    return jnp.where(rows <= half, jnp.cos(phase), jnp.sin(phase)) * scale


def wave_square(index, size):
    half = size // 2
    freq = jnp.where(index <= half, index, index - half).astype(jnp.float32)
    kappa = freq * (2.0 * math.pi / size)
    return kappa * kappa


def interp_matrix(size):
    fine_rows = lax.broadcasted_iota(jnp.int32, (2 * size, size), 0)
    coarse_cols = lax.broadcasted_iota(jnp.int32, (2 * size, size), 1)
    base = fine_rows // 2
    odd = fine_rows % 2
    take_base = jnp.where(coarse_cols == base, jnp.where(odd == 0, 1.0, 0.5), 0.0)
    take_next = jnp.where((odd == 1) & (coarse_cols == (base + 1) % size), 0.5, 0.0)
    return (take_base + take_next).astype(jnp.float32)


def spectral_solve(rhs, basis_x, basis_y, basis_z, factor):
    planes, size_y, size_z = rhs.shape
    flat = jnp.dot(rhs.reshape(planes * size_y, size_z), basis_z.T, precision=HIGHEST)
    field = flat.reshape(planes, size_y, size_z)
    field = jnp.einsum("ky,xyz->kxz", basis_y, field, precision=HIGHEST)
    field = lax.all_to_all(field, "space", split_axis=0, concat_axis=1, tiled=True)
    field = jnp.einsum("kx,yxz->kyz", basis_x, field, precision=HIGHEST) * factor
    field = jnp.einsum("kx,kyz->xyz", basis_x, field, precision=HIGHEST)
    field = lax.all_to_all(field, "space", split_axis=0, concat_axis=1, tiled=True)
    field = jnp.matmul(basis_y.T, field, precision=HIGHEST)
    flat = jnp.dot(field.reshape(planes * size_y, size_z), basis_z, precision=HIGHEST)
    return flat.reshape(planes, size_y, size_z)


def pool_matrix(size):
    rows = lax.broadcasted_iota(jnp.int32, (size // 2, size), 0)
    cells = lax.broadcasted_iota(jnp.int32, (size // 2, size), 1)
    return jnp.where(cells // 2 == rows, 0.5, 0.0).astype(jnp.float32)


def restrict(stacked):
    k, a, b, c = stacked.shape
    planes = stacked.reshape(k, a // 2, 2, b, c)
    planes = 0.5 * (planes[:, :, 0] + planes[:, :, 1])
    half = jnp.einsum("kayz,cz->kayc", planes, pool_matrix(c), precision=HIGHEST)
    return jnp.matmul(pool_matrix(b), half, precision=HIGHEST)


def coarse_rate(stacked):
    padded = extended(stacked, (("space", 1),), 1)
    lap = padded[:, 2:] + padded[:, :-2]
    lap = lap + jnp.roll(stacked, -1, 2) + jnp.roll(stacked, 1, 2)
    lap = lap + jnp.roll(stacked, -1, 3) + jnp.roll(stacked, 1, 3)
    return EPS2 * ((lap - 6.0 * stacked) * 0.25) + react(stacked)


def spread(values, following, axis):
    middle = 0.5 * (values + following)
    both = jnp.stack([values, middle], axis=axis + 1)
    shape = list(values.shape)
    shape[axis] = shape[axis] * 2
    return both.reshape(shape)


def refine(stacked, upper):
    matrix_y = interp_matrix(stacked.shape[2])
    matrix_z = interp_matrix(stacked.shape[3])
    both = jnp.concatenate([stacked, upper], axis=1)
    both = jnp.einsum("kayc,zc->kayz", both, matrix_z, precision=HIGHEST)
    both = jnp.matmul(matrix_y, both, precision=HIGHEST)
    planes = stacked.shape[1]
    return spread(both[:, :planes], both[:, 1:], 1)


def coarse_sweep(start, rates, sums):
    first = start + 0.25 * (coarse_rate(start[None])[0] - rates[0]) + sums[0]
    second = first + 0.25 * (coarse_rate(first[None])[0] - rates[1]) + sums[1]
    return (first, second)


def on_device(fine_nodes, fine_implicit):
    nodes = fine_nodes[0]
    implicit = fine_implicit[0]
    planes, size_y, size_z = (nodes.shape[1], nodes.shape[2], nodes.shape[3])
    devices = lax.axis_size("space")
    size_x = planes * devices
    local_y = size_y // devices
    basis_x = real_basis(size_x)
    basis_y = real_basis(size_y)
    basis_z = real_basis(size_z)
    columns = lax.axis_index("space") * local_y + lax.iota(jnp.int32, local_y)
    lam = wave_square(lax.iota(jnp.int32, size_x), size_x)[:, None, None]
    lam = lam + wave_square(columns, size_y)[None, :, None]
    lam = lam + wave_square(lax.iota(jnp.int32, size_z), size_z)[None, None, :]
    factor = 1.0 / (1.0 + 0.5 * lam)
    explicit_old = react(nodes)
    rates_old = explicit_old + implicit
    values = [nodes[0]]
    terms = [implicit[0]]
    for m in range(2):
        w = WEIGHTS[m]
        quad = 0.5 * (w[0] * rates_old[0] + w[1] * rates_old[1] + w[2] * rates_old[2])
        rhs = (
            values[m] + 0.25 * (react(values[m]) - explicit_old[m]) - 0.25 * implicit[m + 1] + quad
        )
        solved = spectral_solve(rhs, basis_x, basis_y, basis_z, factor)
        values.append(solved)
        terms.append((solved - rhs) * 4.0)
    carried = passed_along(values[2], "tm", 1)
    fresh = jnp.stack(values)
    rates_new = react(fresh) + jnp.stack(terms)
    sums = restrict(
        jnp.stack(
            [
                0.5 * (w[0] * rates_new[0] + w[1] * rates_new[1] + w[2] * rates_new[2])
                for w in WEIGHTS
            ]
        )
    )
    coarse = restrict(fresh)
    rates_c = coarse_rate(coarse[:2])
    slot = lax.axis_index("tm")
    slices = lax.axis_size("tm")
    start = coarse[0]
    for section in range(slices - 1):
        first, second = coarse_sweep(start, rates_c, sums)
        received = passed_along(second, "tm", 1)
        start = jnp.where(slot == 0, coarse[0], received)
    first, second = coarse_sweep(start, rates_c, sums)
    delta = jnp.stack([first - coarse[1], second - coarse[2]])
    upper = shifted(delta[:, :1], "space", -1)
    corr = refine(delta, upper)
    fixed_one = values[1] + corr[0]
    fixed_two = values[2] + corr[1]
    late_delta, late_upper = passed_along((delta[1:], upper[1:]), "tm", 1)
    received_end = carried + refine(late_delta, late_upper)[0]
    head = jnp.where(slot == 0, nodes[0], received_end)
    return (jnp.stack([head, fixed_one, fixed_two])[None], jnp.stack([terms[1], terms[2]])[None])


def solution(mesh):
    return jax.shard_map(
        on_device,
        mesh=mesh,
        in_specs=(P("tm", None, "space", None, None), P("tm", None, "space", None, None)),
        out_specs=(P("tm", None, "space", None, None), P("tm", None, "space", None, None)),
        check_vma=False,
    )
```

```python
import math

import jax
import jax.numpy as jnp
import ml_dtypes
import numpy as np
from jax import lax
from jax.experimental import pallas as pl
from jax.experimental.pallas import tpu as pltpu
from jax.sharding import PartitionSpec as P

WEIGHTS = ((5.0 / 24.0, 1.0 / 3.0, -1.0 / 24.0), (-1.0 / 24.0, 1.0 / 3.0, 5.0 / 24.0))
EPS2 = 2.0
HIGHEST = lax.Precision.HIGHEST


def extended(block, sides, width):
    for axis, dim in sides:
        count = lax.axis_size(axis)
        forward = [(i, i + 1) for i in range(count - 1)]
        forward.append((count - 1, 0))
        backward = [(target, source) for source, target in forward]
        low = lax.ppermute(
            lax.slice_in_dim(block, block.shape[dim] - width, None, axis=dim), axis, forward
        )
        high = lax.ppermute(lax.slice_in_dim(block, 0, width, axis=dim), axis, backward)
        block = jnp.concatenate([low, block, high], axis=dim)
    return block


def passed_along(value, axis, steps):
    count = lax.axis_size(axis)
    leading, last = (max(0, -steps), min(count, count - steps))
    return lax.ppermute(value, axis, [(source, source + steps) for source in range(leading, last)])


def shifted(value, axis, steps):
    count = lax.axis_size(axis)
    pairs = [(source, (source + steps) % count) for source in range(count)]
    return lax.ppermute(value, axis, pairs)


def react(u):
    return u - u * u * u


def real_basis(size):
    rows = lax.broadcasted_iota(jnp.int32, (size, size), 0)
    cells = lax.broadcasted_iota(jnp.int32, (size, size), 1)
    half = size // 2
    freq = jnp.where(rows <= half, rows, rows - half)
    phase = (freq * cells % size).astype(jnp.float32) * (2.0 * math.pi / size)
    scale = jnp.where((rows == 0) | (rows == half), 1.0 / math.sqrt(size), math.sqrt(2.0 / size))
    return jnp.where(rows <= half, jnp.cos(phase), jnp.sin(phase)) * scale


def wave_square(index, size):
    half = size // 2
    freq = jnp.where(index <= half, index, index - half).astype(jnp.float32)
    kappa = freq * (2.0 * math.pi / size)
    return kappa * kappa


def interp_matrix(size):
    fine_rows = lax.broadcasted_iota(jnp.int32, (2 * size, size), 0)
    coarse_cols = lax.broadcasted_iota(jnp.int32, (2 * size, size), 1)
    base = fine_rows // 2
    odd = fine_rows % 2
    take_base = jnp.where(coarse_cols == base, jnp.where(odd == 0, 1.0, 0.5), 0.0)
    take_next = jnp.where((odd == 1) & (coarse_cols == (base + 1) % size), 0.5, 0.0)
    return (take_base + take_next).astype(jnp.float32)


def spectral_solve(rhs, basis_x, basis_y, basis_z, factor):
    planes, size_y, size_z = rhs.shape
    flat = jnp.dot(rhs.reshape(planes * size_y, size_z), basis_z.T, precision=HIGHEST)
    field = flat.reshape(planes, size_y, size_z)
    field = jnp.einsum("ky,xyz->kxz", basis_y, field, precision=HIGHEST)
    field = lax.all_to_all(field, "space", split_axis=0, concat_axis=1, tiled=True)
    field = jnp.einsum("kx,yxz->kyz", basis_x, field, precision=HIGHEST) * factor
    field = jnp.einsum("kx,kyz->xyz", basis_x, field, precision=HIGHEST)
    field = lax.all_to_all(field, "space", split_axis=0, concat_axis=1, tiled=True)
    field = jnp.matmul(basis_y.T, field, precision=HIGHEST)
    flat = jnp.dot(field.reshape(planes * size_y, size_z), basis_z, precision=HIGHEST)
    return flat.reshape(planes, size_y, size_z)


def pool_matrix(size):
    rows = lax.broadcasted_iota(jnp.int32, (size // 2, size), 0)
    cells = lax.broadcasted_iota(jnp.int32, (size // 2, size), 1)
    return jnp.where(cells // 2 == rows, 0.5, 0.0).astype(jnp.float32)


def restrict(stacked):
    k, a, b, c = stacked.shape
    planes = stacked.reshape(k, a // 2, 2, b, c)
    planes = 0.5 * (planes[:, :, 0] + planes[:, :, 1])
    half = jnp.einsum("kayz,cz->kayc", planes, pool_matrix(c), precision=HIGHEST)
    return jnp.matmul(pool_matrix(b), half, precision=HIGHEST)


def coarse_rate(stacked):
    padded = extended(stacked, (("space", 1),), 1)
    lap = padded[:, 2:] + padded[:, :-2]
    lap = lap + jnp.roll(stacked, -1, 2) + jnp.roll(stacked, 1, 2)
    lap = lap + jnp.roll(stacked, -1, 3) + jnp.roll(stacked, 1, 3)
    return EPS2 * ((lap - 6.0 * stacked) * 0.25) + react(stacked)


def spread(values, following, axis):
    middle = 0.5 * (values + following)
    both = jnp.stack([values, middle], axis=axis + 1)
    shape = list(values.shape)
    shape[axis] = shape[axis] * 2
    return both.reshape(shape)


def refine(stacked, upper):
    matrix_y = interp_matrix(stacked.shape[2])
    matrix_z = interp_matrix(stacked.shape[3])
    both = jnp.concatenate([stacked, upper], axis=1)
    both = jnp.einsum("kayc,zc->kayz", both, matrix_z, precision=HIGHEST)
    both = jnp.matmul(matrix_y, both, precision=HIGHEST)
    planes = stacked.shape[1]
    return spread(both[:, :planes], both[:, 1:], 1)


def coarse_sweep(start, rates, sums):
    first = start + 0.25 * (coarse_rate(start[None])[0] - rates[0]) + sums[0]
    second = first + 0.25 * (coarse_rate(first[None])[0] - rates[1]) + sums[1]
    return (first, second)


def on_device(fine_nodes, fine_implicit):
    nodes = fine_nodes[0]
    implicit = fine_implicit[0]
    planes, size_y, size_z = (nodes.shape[1], nodes.shape[2], nodes.shape[3])
    devices = lax.axis_size("space")
    size_x = planes * devices
    local_y = size_y // devices
    basis_x = real_basis(size_x)
    basis_y = real_basis(size_y)
    basis_z = real_basis(size_z)
    columns = lax.axis_index("space") * local_y + lax.iota(jnp.int32, local_y)
    lam = wave_square(lax.iota(jnp.int32, size_x), size_x)[:, None, None]
    lam = lam + wave_square(columns, size_y)[None, :, None]
    lam = lam + wave_square(lax.iota(jnp.int32, size_z), size_z)[None, None, :]
    factor = 1.0 / (1.0 + 0.5 * lam)
    explicit_old = react(nodes)
    rates_old = explicit_old + implicit
    values = [nodes[0]]
    terms = [implicit[0]]
    for m in range(2):
        w = WEIGHTS[m]
        quad = 0.5 * (w[0] * rates_old[0] + w[1] * rates_old[1] + w[2] * rates_old[2])
        rhs = (
            values[m] + 0.25 * (react(values[m]) - explicit_old[m]) - 0.25 * implicit[m + 1] + quad
        )
        solved = spectral_solve(rhs, basis_x, basis_y, basis_z, factor)
        values.append(solved)
        terms.append((solved - rhs) * 4.0)
    carried = passed_along(values[2], "tm", 1)
    fresh = jnp.stack(values)
    rates_new = react(fresh) + jnp.stack(terms)
    sums = restrict(
        jnp.stack(
            [
                0.5 * (w[0] * rates_new[0] + w[1] * rates_new[1] + w[2] * rates_new[2])
                for w in WEIGHTS
            ]
        )
    )
    coarse = restrict(fresh)
    rates_c = coarse_rate(coarse[:2])
    slot = lax.axis_index("tm")
    slices = lax.axis_size("tm")
    start = coarse[0]
    for section in range(slices - 1):
        first, second = coarse_sweep(start, rates_c, sums)
        received = passed_along(second, "tm", 1)
        start = jnp.where(slot == 0, coarse[0], received)
    first, second = coarse_sweep(start, rates_c, sums)
    delta = jnp.stack([first - coarse[1], second - coarse[2]])
    upper = shifted(delta[:, :1], "space", -1)
    corr = refine(delta, upper)
    fixed_one = values[1] + corr[0]
    fixed_two = values[2] + corr[1]
    late_delta, late_upper = passed_along((delta[1:], upper[1:]), "tm", 1)
    received_end = carried + refine(late_delta, late_upper)[0]
    head = jnp.where(slot == 0, nodes[0], received_end)
    return (jnp.stack([head, fixed_one, fixed_two])[None], jnp.stack([terms[1], terms[2]])[None])


BF16 = jnp.bfloat16
F32 = jnp.float32
MESH = pl.DeviceIdType.MESH
CHUNKS = 2
LANES = 128
GROUP = 8
V0, V1, V2, S0, S1 = range(5)


def host_basis(size):
    rows = np.arange(size)[:, None]
    cells = np.arange(size)[None, :]
    half = size // 2
    freq = np.where(rows <= half, rows, rows - half)
    phase = (freq * cells % size) * (2.0 * math.pi / size)
    scale = np.where((rows == 0) | (rows == half), 1.0 / math.sqrt(size), math.sqrt(2.0 / size))
    return np.where(rows <= half, np.cos(phase), np.sin(phase)) * scale


def two_parts(matrix):
    high = matrix.astype(np.float32).astype(ml_dtypes.bfloat16)
    low = (matrix - high.astype(np.float64)).astype(np.float32).astype(ml_dtypes.bfloat16)
    return jnp.asarray(np.stack([high, low]))


def split(value):
    high = value.astype(BF16)
    return high, (value - high.astype(F32)).astype(BF16)


def product(a, b):
    return jnp.dot(a, b, preferred_element_type=F32)


def left(matrix, value):
    high, low = split(value)
    return product(matrix[0], high) + (product(matrix[0], low) + product(matrix[1], high))


def right(value, matrix):
    high, low = split(value)
    return product(high, matrix[0]) + (product(low, matrix[0]) + product(high, matrix[1]))


def right_exact(value, matrix):
    high, low = split(value)
    return product(high, matrix[...]) + product(low, matrix[...])


def rate(value):
    size_y, size_z = value.shape[1:]
    mid = value[1:-1]
    lap = value[2:] + value[:-2]
    lap = lap + pltpu.roll(mid, 1, 1) + pltpu.roll(mid, size_y - 1, 1)
    lap = lap + pltpu.roll(mid, 1, 2) + pltpu.roll(mid, size_z - 1, 2)
    return EPS2 * ((lap - 6.0 * mid) * 0.25) + react(mid)


def kernel(
    nodes, implicit, bz, bzt, bx, bxt, by, byt, pz, iz,
    out_n, out_i,
    send_a, recv_a, send_b, recv_b, passed, factor, pool, ext, va, vb, delta, rows, grid,
    a2a_send, a2a_recv, halo_send, halo_recv, time_send, time_recv,
):
    slot = lax.axis_index("tm")
    me = lax.axis_index("space")
    devices = lax.axis_size("space")
    planes, size_y, size_z = nodes.shape[2:]
    size_x = planes * devices
    block = planes * GROUP

    barrier = pltpu.get_barrier_semaphore()

    def greet(k, carry):
        pl.semaphore_signal(
            barrier, inc=1, device_id=(slot, lax.rem(me + k, devices)), device_id_type=MESH
        )
        return carry

    lax.fori_loop(1, devices, greet, 0)
    pl.semaphore_signal(barrier, inc=1, device_id=(1 - slot, me), device_id_type=MESH)

    def part(index):
        return pl.ds(pl.multiple_of(index * block, block), block)

    def exchange(src, dst, m, c, phase, k):
        target = lax.rem(me + k, devices)
        return pltpu.make_async_remote_copy(
            src_ref=src.at[m, c, part(target)],
            dst_ref=dst.at[m, c, part(me)],
            send_sem=a2a_send.at[phase, c, k],
            recv_sem=a2a_recv.at[phase, c, k],
            device_id=(slot, target),
            device_id_type=MESH,
        )

    def start_all(src, dst, m, c, phase):
        def body(k, carry):
            exchange(src, dst, m, c, phase, k).start()
            return carry

        lax.fori_loop(1, devices, body, 0)
        dst[m, c, part(me), :] = src[m, c, part(me), :]

    def wait_all(src, dst, m, c, phase):
        def body(k, carry):
            exchange(src, dst, m, c, phase, k).wait_recv()
            return carry

        lax.fori_loop(1, devices, body, 0)

    def beside(first, count, low, size, put, step, index):
        return pltpu.make_async_remote_copy(
            src_ref=ext.at[pl.ds(first, count), pl.ds(low, size)],
            dst_ref=ext.at[pl.ds(first, count), pl.ds(put, size)],
            send_sem=halo_send.at[index],
            recv_sem=halo_recv.at[index],
            device_id=(slot, lax.rem(me + step, devices)),
            device_id_type=MESH,
        )

    halos = [
        beside(V0, 1, 5, 3, 1, 1, 0),
        beside(V0, 1, 4, 4, 8, devices - 1, 1),
        beside(V1, 1, 5, 3, 1, 1, 2),
        beside(V1, 1, 4, 4, 8, devices - 1, 3),
        beside(S0, 2, 5, 3, 1, 1, 4),
        beside(S0, 2, 4, 4, 8, devices - 1, 5),
        beside(V2, 1, 4, 1, 8, devices - 1, 6),
    ]

    def ahead(src, dst, index):
        return pltpu.make_async_remote_copy(
            src_ref=src,
            dst_ref=dst,
            send_sem=time_send.at[index],
            recv_sem=time_recv.at[index],
            device_id=(1 - slot, me),
            device_id_type=MESH,
        )

    handed = [ahead(recv_b.at[1, c], passed.at[c], c) for c in range(CHUNKS)]
    handed.append(ahead(vb.at[pl.ds(2, 9)], va.at[pl.ds(2, 9)], CHUNKS))
    handed.append(ahead(delta.at[1], delta.at[2], CHUNKS + 1))

    def quad(m, terms):
        w = WEIGHTS[m]
        return 0.5 * (w[0] * terms[0] + w[1] * terms[1] + w[2] * terms[2])

    def old_rates(x):
        return [react(nodes[0, j, x]) + implicit[0, j, x] for j in range(3)]

    def forward(rhs, x, m):
        field = left(by, right(rhs, bzt))
        for c in range(CHUNKS):
            for d in range(size_y // GROUP):
                send_a[m, c, pl.ds(pl.multiple_of(d * block + x * GROUP, GROUP), GROUP), :] = field[
                    d * GROUP : (d + 1) * GROUP, c * LANES : (c + 1) * LANES
                ]

    def backward(chunk, x):
        field = jnp.concatenate(
            [
                jnp.concatenate(
                    [
                        chunk(c, pl.ds(pl.multiple_of(d * block + x * GROUP, GROUP), GROUP))
                        for d in range(size_y // GROUP)
                    ],
                    axis=0,
                )
                for c in range(CHUNKS)
            ],
            axis=1,
        )
        return right(left(byt, field), bz)

    def first_rhs(x, carry):
        rhs = nodes[0, 0, x] - 0.25 * implicit[0, 1, x] + quad(0, old_rates(x))
        out_i[0, 0, x] = rhs
        forward(rhs, x, 0)
        return carry

    lax.fori_loop(0, planes, first_rhs, 0)
    pl.semaphore_wait(barrier, devices)

    def waves(index, size):
        half = size // 2
        freq = jnp.where(index <= half, index, index - half).astype(F32)
        kappa = freq * (2.0 * math.pi / size)
        return kappa * kappa

    def solve_lines(m, c):
        lines = jnp.concatenate(
            [recv_a[m, c, pl.ds(k, size_x, stride=GROUP), :] for k in range(GROUP)], axis=1
        )
        field = left(bxt, left(bx, lines) * factor[c])
        for k in range(GROUP):
            send_b[m, c, pl.ds(k, size_x, stride=GROUP), :] = field[:, k * LANES : (k + 1) * LANES]

    def average(index, value):
        pool[index] = right_exact(value, pz)
        return 0.5 * (
            pool[index, pl.ds(0, size_y // 2, stride=2), :]
            + pool[index, pl.ds(1, size_y // 2, stride=2), :]
        )

    for c in range(CHUNKS):
        start_all(send_a, recv_a, 0, c, 0)

    shape = (size_x, LANES)
    lam_x = waves(lax.broadcasted_iota(jnp.int32, shape, 0), size_x)
    for c in range(CHUNKS):
        lam_z = waves(lax.broadcasted_iota(jnp.int32, shape, 1) + c * LANES, size_z)
        for k in range(GROUP):
            lam_y = waves(jnp.full(shape, me * GROUP + k, jnp.int32), size_y)
            factor[c, :, k * LANES : (k + 1) * LANES] = 1.0 / (1.0 + 0.5 * (lam_x + lam_y + lam_z))

    def pool_start(p, carry):
        ext[V0, 4 + p] = average(0, 0.5 * (nodes[0, 0, 2 * p] + nodes[0, 0, 2 * p + 1]))
        return carry

    lax.fori_loop(0, planes // 2, pool_start, 0)
    halos[0].start()
    halos[1].start()

    def transfer_lines(m):
        for c in range(CHUNKS):
            wait_all(send_a, recv_a, m, c, 2 * m)
            solve_lines(m, c)
            start_all(send_b, recv_b, m, c, 2 * m + 1)

    transfer_lines(0)
    for c in range(CHUNKS):
        wait_all(send_b, recv_b, 0, c, 1)

    def middle(x, carry):
        solved = backward(lambda c, at: recv_b[0, c, at, :], x)
        term = (solved - out_i[0, 0, x]) * 4.0
        out_n[0, 1, x] = solved
        out_i[0, 0, x] = term
        rhs = (
            solved
            + 0.25 * (react(solved) - react(nodes[0, 1, x]))
            - 0.25 * implicit[0, 2, x]
            + quad(1, old_rates(x))
        )
        out_i[0, 1, x] = rhs
        forward(rhs, x, 1)
        return carry

    lax.fori_loop(0, planes, middle, 0)
    for c in range(CHUNKS):
        start_all(send_a, recv_a, 1, c, 2)

    def pool_middle(p, carry):
        ext[V1, 4 + p] = average(0, 0.5 * (out_n[0, 1, 2 * p] + out_n[0, 1, 2 * p + 1]))
        return carry

    lax.fori_loop(0, planes // 2, pool_middle, 0)
    halos[2].start()
    halos[3].start()

    transfer_lines(1)
    for c in range(CHUNKS):
        wait_all(send_b, recv_b, 1, c, 3)

        @pl.when(slot == 0)
        def _():
            handed[c].start()

    def last(p, carry):
        quads = [0.0, 0.0]
        total = 0.0
        for x in (2 * p, 2 * p + 1):
            solved = backward(lambda c, at: recv_b[1, c, at, :], x)
            term = (solved - out_i[0, 1, x]) * 4.0
            out_n[0, 2, x] = solved
            out_i[0, 1, x] = term
            fresh = [
                react(nodes[0, 0, x]) + implicit[0, 0, x],
                react(out_n[0, 1, x]) + out_i[0, 0, x],
                react(solved) + term,
            ]
            quads = [quads[m] + quad(m, fresh) for m in range(2)]
            total = total + solved
        ext[S0, 4 + p] = average(0, 0.5 * quads[0])
        ext[S1, 4 + p] = average(1, 0.5 * quads[1])
        ext[V2, 4 + p] = average(2, 0.5 * total)
        return carry

    lax.fori_loop(0, planes // 2, last, 0)
    for halo in halos[4:]:
        halo.start()
    for halo in halos:
        halo.wait_recv()

    @pl.when(slot == 0)
    def _():
        first = ext[V0, 1:12] + ext[S0, 1:12]
        second = first[1:-1] + 0.25 * (rate(first) - rate(ext[V1, 1:12])) + ext[S1, 2:11]
        vb[2:11] = second
        handed[CHUNKS].start()
        delta[0] = first[3:8] - ext[V1, 4:9]
        delta[1] = second[2:7] - ext[V2, 4:9]
        handed[CHUNKS + 1].start()

    @pl.when(slot == 1)
    def _():
        handed[CHUNKS].wait_recv()
        begin = va[2:11]
        first = begin[1:-1] + 0.25 * (rate(begin) - rate(ext[V0, 2:11])) + ext[S0, 3:10]
        second = first[1:-1] + 0.25 * (rate(first) - rate(ext[V1, 3:10])) + ext[S1, 4:9]
        delta[0] = first[1:6] - ext[V1, 4:9]
        delta[1] = second - ext[V2, 4:9]

    def refined(index):
        def body(p, carry):
            coarse = delta[index, p]
            rows[pl.ds(0, size_y // 2, stride=2), :] = coarse
            rows[pl.ds(1, size_y // 2, stride=2), :] = 0.5 * (
                coarse + pltpu.roll(coarse, size_y // 2 - 1, 0)
            )
            grid[p] = right_exact(rows[...], iz)
            return carry

        lax.fori_loop(0, planes // 2 + 1, body, 0)

    def correct(index, base, target):
        refined(index)

        def body(p, carry):
            out_n[0, target, 2 * p] = base(2 * p) + grid[p]
            out_n[0, target, 2 * p + 1] = base(2 * p + 1) + 0.5 * (grid[p] + grid[p + 1])
            return carry

        lax.fori_loop(0, planes // 2, body, 0)

    correct(0, lambda x: out_n[0, 1, x], 1)
    correct(1, lambda x: out_n[0, 2, x], 2)

    @pl.when(slot == 0)
    def _():
        out_n[0, 0] = nodes[0, 0]
        for copy in handed:
            copy.wait_send()

    @pl.when(slot == 1)
    def _():
        for c in range(CHUNKS):
            handed[c].wait_recv()

        handed[CHUNKS + 1].wait_recv()
        correct(2, lambda x: backward(lambda c, at: passed[c, at, :], x), 0)

    for phase, (src, dst) in enumerate([(send_a, recv_a), (send_b, recv_b)] * 2):
        for c in range(CHUNKS):

            def body(k, carry, src=src, dst=dst, phase=phase, c=c):
                exchange(src, dst, phase // 2, c, phase, k).wait_send()
                return carry

            lax.fori_loop(1, devices, body, 0)
    for halo in halos:
        halo.wait_send()


def fused(fine_nodes, fine_implicit):
    planes, size_y, size_z = fine_nodes.shape[2:]
    devices = lax.axis_size("space")
    basis_x = host_basis(planes * devices)
    basis_y = host_basis(size_y)
    basis_z = host_basis(size_z)
    cells = np.arange(size_z)
    half = np.zeros((size_z, size_z // 2))
    half[cells, cells // 2] = 0.5
    lines = np.zeros((size_z // 2, size_z))
    coarse = np.arange(size_z // 2)
    lines[coarse, 2 * coarse] = 1.0
    lines[coarse, 2 * coarse + 1] += 0.5
    lines[(coarse + 1) % (size_z // 2), 2 * coarse + 1] += 0.5
    constants = [
        two_parts(m) for m in (basis_z, basis_z.T, basis_x, basis_x.T, basis_y, basis_y.T)
    ]
    constants.append(jnp.asarray(half.astype(ml_dtypes.bfloat16)))
    constants.append(jnp.asarray(lines.astype(ml_dtypes.bfloat16)))
    field = (2, CHUNKS, devices * planes * GROUP, LANES)
    plane = (size_y // 2, size_z // 2)
    vmem = pl.BlockSpec(memory_space=pltpu.VMEM)
    shape_n = fine_nodes.shape
    shape_i = shape_n[:1] + (2,) + shape_n[2:]
    return pl.pallas_call(
        kernel,
        out_shape=(jax.ShapeDtypeStruct(shape_n, F32), jax.ShapeDtypeStruct(shape_i, F32)),
        in_specs=[vmem] * 10,
        out_specs=(vmem, vmem),
        scratch_shapes=[
            pltpu.VMEM(field, F32),
            pltpu.VMEM(field, F32),
            pltpu.VMEM(field, F32),
            pltpu.VMEM(field, F32),
            pltpu.VMEM(field[1:], F32),
            pltpu.VMEM((CHUNKS, planes * devices, GROUP * LANES), F32),
            pltpu.VMEM((3, size_y, size_z // 2), F32),
            pltpu.VMEM((5, 12) + plane, F32),
            pltpu.VMEM((12,) + plane, F32),
            pltpu.VMEM((12,) + plane, F32),
            pltpu.VMEM((3, 5) + plane, F32),
            pltpu.VMEM((size_y, size_z // 2), F32),
            pltpu.VMEM((5, size_y, size_z), F32),
            pltpu.SemaphoreType.DMA((4, CHUNKS, devices)),
            pltpu.SemaphoreType.DMA((4, CHUNKS, devices)),
            pltpu.SemaphoreType.DMA((7,)),
            pltpu.SemaphoreType.DMA((7,)),
            pltpu.SemaphoreType.DMA((CHUNKS + 2,)),
            pltpu.SemaphoreType.DMA((CHUNKS + 2,)),
        ],
        compiler_params=pltpu.CompilerParams(
            collective_id=0, has_side_effects=True, vmem_limit_bytes=56 * 2**20
        ),
    )(fine_nodes, fine_implicit, *constants)


def either(fine_nodes, fine_implicit):
    planes, size_y, size_z = fine_nodes.shape[2:]
    devices = lax.axis_size("space")
    fits = planes == GROUP and size_y == GROUP * devices and size_z == CHUNKS * LANES
    if fits and lax.axis_size("tm") == 2:
        return fused(fine_nodes, fine_implicit)
    return on_device(fine_nodes, fine_implicit)


def solution(mesh):
    return jax.shard_map(
        either,
        mesh=mesh,
        in_specs=(P("tm", None, "space", None, None), P("tm", None, "space", None, None)),
        out_specs=(P("tm", None, "space", None, None), P("tm", None, "space", None, None)),
        check_vma=False,
    )
```

```python
import math

import jax
import jax.numpy as jnp
import ml_dtypes
import numpy as np
from jax import lax
from jax.experimental import pallas as pl
from jax.experimental.pallas import tpu as pltpu
from jax.sharding import PartitionSpec as P

WEIGHTS = ((5.0 / 24.0, 1.0 / 3.0, -1.0 / 24.0), (-1.0 / 24.0, 1.0 / 3.0, 5.0 / 24.0))
EPS2 = 2.0
HIGHEST = lax.Precision.HIGHEST


def extended(block, sides, width):
    for axis, dim in sides:
        count = lax.axis_size(axis)
        forward = [(i, i + 1) for i in range(count - 1)]
        forward.append((count - 1, 0))
        backward = [(target, source) for source, target in forward]
        low = lax.ppermute(
            lax.slice_in_dim(block, block.shape[dim] - width, None, axis=dim), axis, forward
        )
        high = lax.ppermute(lax.slice_in_dim(block, 0, width, axis=dim), axis, backward)
        block = jnp.concatenate([low, block, high], axis=dim)
    return block


def passed_along(value, axis, steps):
    count = lax.axis_size(axis)
    leading, last = (max(0, -steps), min(count, count - steps))
    return lax.ppermute(value, axis, [(source, source + steps) for source in range(leading, last)])


def shifted(value, axis, steps):
    count = lax.axis_size(axis)
    pairs = [(source, (source + steps) % count) for source in range(count)]
    return lax.ppermute(value, axis, pairs)


def react(u):
    return u - u * u * u


def real_basis(size):
    rows = lax.broadcasted_iota(jnp.int32, (size, size), 0)
    cells = lax.broadcasted_iota(jnp.int32, (size, size), 1)
    half = size // 2
    freq = jnp.where(rows <= half, rows, rows - half)
    phase = (freq * cells % size).astype(jnp.float32) * (2.0 * math.pi / size)
    scale = jnp.where((rows == 0) | (rows == half), 1.0 / math.sqrt(size), math.sqrt(2.0 / size))
    return jnp.where(rows <= half, jnp.cos(phase), jnp.sin(phase)) * scale


def wave_square(index, size):
    half = size // 2
    freq = jnp.where(index <= half, index, index - half).astype(jnp.float32)
    kappa = freq * (2.0 * math.pi / size)
    return kappa * kappa


def interp_matrix(size):
    fine_rows = lax.broadcasted_iota(jnp.int32, (2 * size, size), 0)
    coarse_cols = lax.broadcasted_iota(jnp.int32, (2 * size, size), 1)
    base = fine_rows // 2
    odd = fine_rows % 2
    take_base = jnp.where(coarse_cols == base, jnp.where(odd == 0, 1.0, 0.5), 0.0)
    take_next = jnp.where((odd == 1) & (coarse_cols == (base + 1) % size), 0.5, 0.0)
    return (take_base + take_next).astype(jnp.float32)


def spectral_solve(rhs, basis_x, basis_y, basis_z, factor):
    planes, size_y, size_z = rhs.shape
    flat = jnp.dot(rhs.reshape(planes * size_y, size_z), basis_z.T, precision=HIGHEST)
    field = flat.reshape(planes, size_y, size_z)
    field = jnp.einsum("ky,xyz->kxz", basis_y, field, precision=HIGHEST)
    field = lax.all_to_all(field, "space", split_axis=0, concat_axis=1, tiled=True)
    field = jnp.einsum("kx,yxz->kyz", basis_x, field, precision=HIGHEST) * factor
    field = jnp.einsum("kx,kyz->xyz", basis_x, field, precision=HIGHEST)
    field = lax.all_to_all(field, "space", split_axis=0, concat_axis=1, tiled=True)
    field = jnp.matmul(basis_y.T, field, precision=HIGHEST)
    flat = jnp.dot(field.reshape(planes * size_y, size_z), basis_z, precision=HIGHEST)
    return flat.reshape(planes, size_y, size_z)


def pool_matrix(size):
    rows = lax.broadcasted_iota(jnp.int32, (size // 2, size), 0)
    cells = lax.broadcasted_iota(jnp.int32, (size // 2, size), 1)
    return jnp.where(cells // 2 == rows, 0.5, 0.0).astype(jnp.float32)


def restrict(stacked):
    k, a, b, c = stacked.shape
    planes = stacked.reshape(k, a // 2, 2, b, c)
    planes = 0.5 * (planes[:, :, 0] + planes[:, :, 1])
    half = jnp.einsum("kayz,cz->kayc", planes, pool_matrix(c), precision=HIGHEST)
    return jnp.matmul(pool_matrix(b), half, precision=HIGHEST)


def coarse_rate(stacked):
    padded = extended(stacked, (("space", 1),), 1)
    lap = padded[:, 2:] + padded[:, :-2]
    lap = lap + jnp.roll(stacked, -1, 2) + jnp.roll(stacked, 1, 2)
    lap = lap + jnp.roll(stacked, -1, 3) + jnp.roll(stacked, 1, 3)
    return EPS2 * ((lap - 6.0 * stacked) * 0.25) + react(stacked)


def spread(values, following, axis):
    middle = 0.5 * (values + following)
    both = jnp.stack([values, middle], axis=axis + 1)
    shape = list(values.shape)
    shape[axis] = shape[axis] * 2
    return both.reshape(shape)


def refine(stacked, upper):
    matrix_y = interp_matrix(stacked.shape[2])
    matrix_z = interp_matrix(stacked.shape[3])
    both = jnp.concatenate([stacked, upper], axis=1)
    both = jnp.einsum("kayc,zc->kayz", both, matrix_z, precision=HIGHEST)
    both = jnp.matmul(matrix_y, both, precision=HIGHEST)
    planes = stacked.shape[1]
    return spread(both[:, :planes], both[:, 1:], 1)


def coarse_sweep(start, rates, sums):
    first = start + 0.25 * (coarse_rate(start[None])[0] - rates[0]) + sums[0]
    second = first + 0.25 * (coarse_rate(first[None])[0] - rates[1]) + sums[1]
    return (first, second)


def on_device(fine_nodes, fine_implicit):
    nodes = fine_nodes[0]
    implicit = fine_implicit[0]
    planes, size_y, size_z = (nodes.shape[1], nodes.shape[2], nodes.shape[3])
    devices = lax.axis_size("space")
    size_x = planes * devices
    local_y = size_y // devices
    basis_x = real_basis(size_x)
    basis_y = real_basis(size_y)
    basis_z = real_basis(size_z)
    columns = lax.axis_index("space") * local_y + lax.iota(jnp.int32, local_y)
    lam = wave_square(lax.iota(jnp.int32, size_x), size_x)[:, None, None]
    lam = lam + wave_square(columns, size_y)[None, :, None]
    lam = lam + wave_square(lax.iota(jnp.int32, size_z), size_z)[None, None, :]
    factor = 1.0 / (1.0 + 0.5 * lam)
    explicit_old = react(nodes)
    rates_old = explicit_old + implicit
    values = [nodes[0]]
    terms = [implicit[0]]
    for m in range(2):
        w = WEIGHTS[m]
        quad = 0.5 * (w[0] * rates_old[0] + w[1] * rates_old[1] + w[2] * rates_old[2])
        rhs = (
            values[m] + 0.25 * (react(values[m]) - explicit_old[m]) - 0.25 * implicit[m + 1] + quad
        )
        solved = spectral_solve(rhs, basis_x, basis_y, basis_z, factor)
        values.append(solved)
        terms.append((solved - rhs) * 4.0)
    carried = passed_along(values[2], "tm", 1)
    fresh = jnp.stack(values)
    rates_new = react(fresh) + jnp.stack(terms)
    sums = restrict(
        jnp.stack(
            [
                0.5 * (w[0] * rates_new[0] + w[1] * rates_new[1] + w[2] * rates_new[2])
                for w in WEIGHTS
            ]
        )
    )
    coarse = restrict(fresh)
    rates_c = coarse_rate(coarse[:2])
    slot = lax.axis_index("tm")
    slices = lax.axis_size("tm")
    start = coarse[0]
    for section in range(slices - 1):
        first, second = coarse_sweep(start, rates_c, sums)
        received = passed_along(second, "tm", 1)
        start = jnp.where(slot == 0, coarse[0], received)
    first, second = coarse_sweep(start, rates_c, sums)
    delta = jnp.stack([first - coarse[1], second - coarse[2]])
    upper = shifted(delta[:, :1], "space", -1)
    corr = refine(delta, upper)
    fixed_one = values[1] + corr[0]
    fixed_two = values[2] + corr[1]
    late_delta, late_upper = passed_along((delta[1:], upper[1:]), "tm", 1)
    received_end = carried + refine(late_delta, late_upper)[0]
    head = jnp.where(slot == 0, nodes[0], received_end)
    return (jnp.stack([head, fixed_one, fixed_two])[None], jnp.stack([terms[1], terms[2]])[None])


BF16 = jnp.bfloat16
F32 = jnp.float32
MESH = pl.DeviceIdType.MESH
CHUNKS = 2
LANES = 128
GROUP = 8
V0, V1, V2, S0, S1 = range(5)


def host_basis(size):
    rows = np.arange(size)[:, None]
    cells = np.arange(size)[None, :]
    half = size // 2
    freq = np.where(rows <= half, rows, rows - half)
    phase = (freq * cells % size) * (2.0 * math.pi / size)
    scale = np.where((rows == 0) | (rows == half), 1.0 / math.sqrt(size), math.sqrt(2.0 / size))
    return np.where(rows <= half, np.cos(phase), np.sin(phase)) * scale


def two_parts(matrix):
    high = matrix.astype(np.float32).astype(ml_dtypes.bfloat16)
    low = (matrix - high.astype(np.float64)).astype(np.float32).astype(ml_dtypes.bfloat16)
    return jnp.asarray(np.stack([high, low]))


def split(value):
    high = value.astype(BF16)
    return high, (value - high.astype(F32)).astype(BF16)


def product(a, b):
    return jnp.dot(a, b, preferred_element_type=F32)


def left(matrix, value):
    high, low = split(value)
    return product(matrix[0], high) + (product(matrix[0], low) + product(matrix[1], high))


def right(value, matrix):
    high, low = split(value)
    return product(high, matrix[0]) + (product(low, matrix[0]) + product(high, matrix[1]))


def right_exact(value, matrix):
    high, low = split(value)
    return product(high, matrix[...]) + product(low, matrix[...])


def rate(value):
    size_y, size_z = value.shape[1:]
    mid = value[1:-1]
    lap = value[2:] + value[:-2]
    lap = lap + pltpu.roll(mid, 1, 1) + pltpu.roll(mid, size_y - 1, 1)
    lap = lap + pltpu.roll(mid, 1, 2) + pltpu.roll(mid, size_z - 1, 2)
    return EPS2 * ((lap - 6.0 * mid) * 0.25) + react(mid)


def kernel(
    nodes, implicit, bz, bzt, bx, bxt, by, byt, pz, iz,
    out_n, out_i,
    send_a, recv_a, send_b, recv_b, passed, factor, pool, ext, va, vb, delta, rows, grid, early,
    a2a_send, a2a_recv, halo_send, halo_recv, time_send, time_recv,
):
    slot = lax.axis_index("tm")
    me = lax.axis_index("space")
    devices = lax.axis_size("space")
    planes, size_y, size_z = nodes.shape[2:]
    size_x = planes * devices
    block = planes * GROUP

    barrier = pltpu.get_barrier_semaphore()

    def greet(k, carry):
        pl.semaphore_signal(
            barrier, inc=1, device_id=(slot, lax.rem(me + k, devices)), device_id_type=MESH
        )
        return carry

    lax.fori_loop(1, devices, greet, 0)
    pl.semaphore_signal(barrier, inc=1, device_id=(1 - slot, me), device_id_type=MESH)

    def part(index):
        return pl.ds(pl.multiple_of(index * block, block), block)

    def exchange(src, dst, m, c, phase, k):
        target = lax.rem(me + k, devices)
        return pltpu.make_async_remote_copy(
            src_ref=src.at[m, c, part(target)],
            dst_ref=dst.at[m, c, part(me)],
            send_sem=a2a_send.at[phase, c, k],
            recv_sem=a2a_recv.at[phase, c, k],
            device_id=(slot, target),
            device_id_type=MESH,
        )

    def start_all(src, dst, m, c, phase):
        def body(k, carry):
            exchange(src, dst, m, c, phase, k).start()
            return carry

        lax.fori_loop(1, devices, body, 0)
        dst[m, c, part(me), :] = src[m, c, part(me), :]

    def wait_all(src, dst, m, c, phase):
        def body(k, carry):
            exchange(src, dst, m, c, phase, k).wait_recv()
            return carry

        lax.fori_loop(1, devices, body, 0)

    def beside(first, count, low, size, put, step, index):
        return pltpu.make_async_remote_copy(
            src_ref=ext.at[pl.ds(first, count), pl.ds(low, size)],
            dst_ref=ext.at[pl.ds(first, count), pl.ds(put, size)],
            send_sem=halo_send.at[index],
            recv_sem=halo_recv.at[index],
            device_id=(slot, lax.rem(me + step, devices)),
            device_id_type=MESH,
        )

    halos = [
        beside(V0, 1, 5, 3, 1, 1, 0),
        beside(V0, 1, 4, 4, 8, devices - 1, 1),
        beside(V1, 1, 5, 3, 1, 1, 2),
        beside(V1, 1, 4, 4, 8, devices - 1, 3),
        beside(S0, 2, 5, 3, 1, 1, 4),
        beside(S0, 2, 4, 4, 8, devices - 1, 5),
        beside(V2, 1, 4, 1, 8, devices - 1, 6),
    ]

    def ahead(src, dst, index):
        return pltpu.make_async_remote_copy(
            src_ref=src,
            dst_ref=dst,
            send_sem=time_send.at[index],
            recv_sem=time_recv.at[index],
            device_id=(1 - slot, me),
            device_id_type=MESH,
        )

    handed = [ahead(recv_b.at[1, c], passed.at[c], c) for c in range(CHUNKS)]
    handed.append(ahead(vb.at[pl.ds(2, 9)], va.at[pl.ds(2, 9)], CHUNKS))
    handed.append(ahead(delta.at[1], delta.at[2], CHUNKS + 1))

    def quad(m, terms):
        w = WEIGHTS[m]
        return 0.5 * (w[0] * terms[0] + w[1] * terms[1] + w[2] * terms[2])

    def old_rates(x):
        return [react(nodes[0, j, x]) + implicit[0, j, x] for j in range(3)]

    def forward(rhs, x, m):
        field = left(by, right(rhs, bzt))
        for c in range(CHUNKS):
            for d in range(size_y // GROUP):
                send_a[m, c, pl.ds(pl.multiple_of(d * block + x * GROUP, GROUP), GROUP), :] = field[
                    d * GROUP : (d + 1) * GROUP, c * LANES : (c + 1) * LANES
                ]

    def undo(chunk, c, x):
        return left(
            byt,
            jnp.concatenate(
                [
                    chunk(c, pl.ds(pl.multiple_of(d * block + x * GROUP, GROUP), GROUP))
                    for d in range(size_y // GROUP)
                ],
                axis=0,
            ),
        )

    def prepare(chunk):
        def body(x, carry):
            early[x] = undo(chunk, 0, x)
            return carry

        lax.fori_loop(0, planes, body, 0, unroll=4)

    def backward(chunk, x):
        return right(jnp.concatenate([early[x], undo(chunk, 1, x)], axis=1), bz)

    def first_rhs(x, carry):
        rhs = nodes[0, 0, x] - 0.25 * implicit[0, 1, x] + quad(0, old_rates(x))
        out_i[0, 0, x] = rhs
        forward(rhs, x, 0)
        return carry

    lax.fori_loop(0, planes, first_rhs, 0, unroll=4)
    pl.semaphore_wait(barrier, devices)

    def waves(index, size):
        half = size // 2
        freq = jnp.where(index <= half, index, index - half).astype(F32)
        kappa = freq * (2.0 * math.pi / size)
        return kappa * kappa

    def solve_lines(m, c):
        lines = jnp.concatenate(
            [recv_a[m, c, pl.ds(k, size_x, stride=GROUP), :] for k in range(GROUP)], axis=1
        )
        field = left(bxt, left(bx, lines) * factor[c])
        for k in range(GROUP):
            send_b[m, c, pl.ds(k, size_x, stride=GROUP), :] = field[:, k * LANES : (k + 1) * LANES]

    def average(index, value):
        pool[index] = right_exact(value, pz)
        return 0.5 * (
            pool[index, pl.ds(0, size_y // 2, stride=2), :]
            + pool[index, pl.ds(1, size_y // 2, stride=2), :]
        )

    for c in range(CHUNKS):
        start_all(send_a, recv_a, 0, c, 0)

    shape = (size_x, LANES)
    lam_x = waves(lax.broadcasted_iota(jnp.int32, shape, 0), size_x)
    for c in range(CHUNKS):
        lam_z = waves(lax.broadcasted_iota(jnp.int32, shape, 1) + c * LANES, size_z)
        for k in range(GROUP):
            lam_y = waves(jnp.full(shape, me * GROUP + k, jnp.int32), size_y)
            factor[c, :, k * LANES : (k + 1) * LANES] = 1.0 / (1.0 + 0.5 * (lam_x + lam_y + lam_z))

    def pool_start(p, carry):
        ext[V0, 4 + p] = average(0, 0.5 * (nodes[0, 0, 2 * p] + nodes[0, 0, 2 * p + 1]))
        return carry

    lax.fori_loop(0, planes // 2, pool_start, 0)
    halos[0].start()
    halos[1].start()

    def transfer_lines(m):
        for c in range(CHUNKS):
            wait_all(send_a, recv_a, m, c, 2 * m)
            solve_lines(m, c)
            start_all(send_b, recv_b, m, c, 2 * m + 1)

    transfer_lines(0)
    for c in range(CHUNKS):
        wait_all(send_b, recv_b, 0, c, 1)
        if c == 0:
            prepare(lambda c, at: recv_b[0, c, at, :])

    def middle(x, carry):
        solved = backward(lambda c, at: recv_b[0, c, at, :], x)
        term = (solved - out_i[0, 0, x]) * 4.0
        out_n[0, 1, x] = solved
        out_i[0, 0, x] = term
        rhs = (
            solved
            + 0.25 * (react(solved) - react(nodes[0, 1, x]))
            - 0.25 * implicit[0, 2, x]
            + quad(1, old_rates(x))
        )
        out_i[0, 1, x] = rhs
        forward(rhs, x, 1)
        return carry

    lax.fori_loop(0, planes, middle, 0, unroll=4)
    for c in range(CHUNKS):
        start_all(send_a, recv_a, 1, c, 2)

    def pool_middle(p, carry):
        ext[V1, 4 + p] = average(0, 0.5 * (out_n[0, 1, 2 * p] + out_n[0, 1, 2 * p + 1]))
        return carry

    lax.fori_loop(0, planes // 2, pool_middle, 0)
    halos[2].start()
    halos[3].start()

    transfer_lines(1)
    for c in range(CHUNKS):
        wait_all(send_b, recv_b, 1, c, 3)

        @pl.when(slot == 0)
        def _():
            handed[c].start()

        if c == 0:
            prepare(lambda c, at: recv_b[1, c, at, :])

    def last(p, carry):
        quads = [0.0, 0.0]
        total = 0.0
        for x in (2 * p, 2 * p + 1):
            solved = backward(lambda c, at: recv_b[1, c, at, :], x)
            term = (solved - out_i[0, 1, x]) * 4.0
            out_n[0, 2, x] = solved
            out_i[0, 1, x] = term
            fresh = [
                react(nodes[0, 0, x]) + implicit[0, 0, x],
                react(out_n[0, 1, x]) + out_i[0, 0, x],
                react(solved) + term,
            ]
            quads = [quads[m] + quad(m, fresh) for m in range(2)]
            total = total + solved
        ext[S0, 4 + p] = average(0, 0.5 * quads[0])
        ext[S1, 4 + p] = average(1, 0.5 * quads[1])
        ext[V2, 4 + p] = average(2, 0.5 * total)
        return carry

    lax.fori_loop(0, planes // 2, last, 0, unroll=2)
    for halo in halos[4:]:
        halo.start()
    for halo in halos:
        halo.wait_recv()

    @pl.when(slot == 0)
    def _():
        first = ext[V0, 1:12] + ext[S0, 1:12]
        second = first[1:-1] + 0.25 * (rate(first) - rate(ext[V1, 1:12])) + ext[S1, 2:11]
        vb[2:11] = second
        handed[CHUNKS].start()
        delta[0] = first[3:8] - ext[V1, 4:9]
        delta[1] = second[2:7] - ext[V2, 4:9]
        handed[CHUNKS + 1].start()

    @pl.when(slot == 1)
    def _():
        handed[CHUNKS].wait_recv()
        begin = va[2:11]
        first = begin[1:-1] + 0.25 * (rate(begin) - rate(ext[V0, 2:11])) + ext[S0, 3:10]
        second = first[1:-1] + 0.25 * (rate(first) - rate(ext[V1, 3:10])) + ext[S1, 4:9]
        delta[0] = first[1:6] - ext[V1, 4:9]
        delta[1] = second - ext[V2, 4:9]

    def refined(index):
        def body(p, carry):
            coarse = delta[index, p]
            rows[pl.ds(0, size_y // 2, stride=2), :] = coarse
            rows[pl.ds(1, size_y // 2, stride=2), :] = 0.5 * (
                coarse + pltpu.roll(coarse, size_y // 2 - 1, 0)
            )
            grid[p] = right_exact(rows[...], iz)
            return carry

        lax.fori_loop(0, planes // 2 + 1, body, 0)

    def correct(index, base, target):
        refined(index)

        def body(p, carry):
            out_n[0, target, 2 * p] = base(2 * p) + grid[p]
            out_n[0, target, 2 * p + 1] = base(2 * p + 1) + 0.5 * (grid[p] + grid[p + 1])
            return carry

        lax.fori_loop(0, planes // 2, body, 0, unroll=2)

    correct(0, lambda x: out_n[0, 1, x], 1)
    correct(1, lambda x: out_n[0, 2, x], 2)

    @pl.when(slot == 0)
    def _():
        out_n[0, 0] = nodes[0, 0]
        for copy in handed:
            copy.wait_send()

    @pl.when(slot == 1)
    def _():
        for c in range(CHUNKS):
            handed[c].wait_recv()
            if c == 0:
                prepare(lambda c, at: passed[c, at, :])

        handed[CHUNKS + 1].wait_recv()
        correct(2, lambda x: backward(lambda c, at: passed[c, at, :], x), 0)

    for phase, (src, dst) in enumerate([(send_a, recv_a), (send_b, recv_b)] * 2):
        for c in range(CHUNKS):

            def body(k, carry, src=src, dst=dst, phase=phase, c=c):
                exchange(src, dst, phase // 2, c, phase, k).wait_send()
                return carry

            lax.fori_loop(1, devices, body, 0)
    for halo in halos:
        halo.wait_send()


def fused(fine_nodes, fine_implicit):
    planes, size_y, size_z = fine_nodes.shape[2:]
    devices = lax.axis_size("space")
    basis_x = host_basis(planes * devices)
    basis_y = host_basis(size_y)
    basis_z = host_basis(size_z)
    cells = np.arange(size_z)
    half = np.zeros((size_z, size_z // 2))
    half[cells, cells // 2] = 0.5
    lines = np.zeros((size_z // 2, size_z))
    coarse = np.arange(size_z // 2)
    lines[coarse, 2 * coarse] = 1.0
    lines[coarse, 2 * coarse + 1] += 0.5
    lines[(coarse + 1) % (size_z // 2), 2 * coarse + 1] += 0.5
    constants = [
        two_parts(m) for m in (basis_z, basis_z.T, basis_x, basis_x.T, basis_y, basis_y.T)
    ]
    constants.append(jnp.asarray(half.astype(ml_dtypes.bfloat16)))
    constants.append(jnp.asarray(lines.astype(ml_dtypes.bfloat16)))
    field = (2, CHUNKS, devices * planes * GROUP, LANES)
    plane = (size_y // 2, size_z // 2)
    vmem = pl.BlockSpec(memory_space=pltpu.VMEM)
    shape_n = fine_nodes.shape
    shape_i = shape_n[:1] + (2,) + shape_n[2:]
    return pl.pallas_call(
        kernel,
        out_shape=(jax.ShapeDtypeStruct(shape_n, F32), jax.ShapeDtypeStruct(shape_i, F32)),
        in_specs=[vmem] * 10,
        out_specs=(vmem, vmem),
        scratch_shapes=[
            pltpu.VMEM(field, F32),
            pltpu.VMEM(field, F32),
            pltpu.VMEM(field, F32),
            pltpu.VMEM(field, F32),
            pltpu.VMEM(field[1:], F32),
            pltpu.VMEM((CHUNKS, planes * devices, GROUP * LANES), F32),
            pltpu.VMEM((3, size_y, size_z // 2), F32),
            pltpu.VMEM((5, 12) + plane, F32),
            pltpu.VMEM((12,) + plane, F32),
            pltpu.VMEM((12,) + plane, F32),
            pltpu.VMEM((3, 5) + plane, F32),
            pltpu.VMEM((size_y, size_z // 2), F32),
            pltpu.VMEM((5, size_y, size_z), F32),
            pltpu.VMEM((planes, size_y, LANES), F32),
            pltpu.SemaphoreType.DMA((4, CHUNKS, devices)),
            pltpu.SemaphoreType.DMA((4, CHUNKS, devices)),
            pltpu.SemaphoreType.DMA((7,)),
            pltpu.SemaphoreType.DMA((7,)),
            pltpu.SemaphoreType.DMA((CHUNKS + 2,)),
            pltpu.SemaphoreType.DMA((CHUNKS + 2,)),
        ],
        compiler_params=pltpu.CompilerParams(
            collective_id=0, has_side_effects=True, vmem_limit_bytes=56 * 2**20
        ),
    )(fine_nodes, fine_implicit, *constants)


def either(fine_nodes, fine_implicit):
    planes, size_y, size_z = fine_nodes.shape[2:]
    devices = lax.axis_size("space")
    fits = planes == GROUP and size_y == GROUP * devices and size_z == CHUNKS * LANES
    if fits and lax.axis_size("tm") == 2:
        return fused(fine_nodes, fine_implicit)
    return on_device(fine_nodes, fine_implicit)


def solution(mesh):
    return jax.shard_map(
        either,
        mesh=mesh,
        in_specs=(P("tm", None, "space", None, None), P("tm", None, "space", None, None)),
        out_specs=(P("tm", None, "space", None, None), P("tm", None, "space", None, None)),
        check_vma=False,
    )
```

```python
import math

import jax
import jax.numpy as jnp
import ml_dtypes
import numpy as np
from jax import lax
from jax.experimental import pallas as pl
from jax.experimental.pallas import tpu as pltpu
from jax.sharding import PartitionSpec as P

WEIGHTS = ((5.0 / 24.0, 1.0 / 3.0, -1.0 / 24.0), (-1.0 / 24.0, 1.0 / 3.0, 5.0 / 24.0))
EPS2 = 2.0
HIGHEST = lax.Precision.HIGHEST


def extended(block, sides, width):
    for axis, dim in sides:
        count = lax.axis_size(axis)
        forward = [(i, i + 1) for i in range(count - 1)]
        forward.append((count - 1, 0))
        backward = [(target, source) for source, target in forward]
        low = lax.ppermute(
            lax.slice_in_dim(block, block.shape[dim] - width, None, axis=dim), axis, forward
        )
        high = lax.ppermute(lax.slice_in_dim(block, 0, width, axis=dim), axis, backward)
        block = jnp.concatenate([low, block, high], axis=dim)
    return block


def passed_along(value, axis, steps):
    count = lax.axis_size(axis)
    leading, last = (max(0, -steps), min(count, count - steps))
    return lax.ppermute(value, axis, [(source, source + steps) for source in range(leading, last)])


def shifted(value, axis, steps):
    count = lax.axis_size(axis)
    pairs = [(source, (source + steps) % count) for source in range(count)]
    return lax.ppermute(value, axis, pairs)


def react(u):
    return u - u * u * u


def real_basis(size):
    rows = lax.broadcasted_iota(jnp.int32, (size, size), 0)
    cells = lax.broadcasted_iota(jnp.int32, (size, size), 1)
    half = size // 2
    freq = jnp.where(rows <= half, rows, rows - half)
    phase = (freq * cells % size).astype(jnp.float32) * (2.0 * math.pi / size)
    scale = jnp.where((rows == 0) | (rows == half), 1.0 / math.sqrt(size), math.sqrt(2.0 / size))
    return jnp.where(rows <= half, jnp.cos(phase), jnp.sin(phase)) * scale


def wave_square(index, size):
    half = size // 2
    freq = jnp.where(index <= half, index, index - half).astype(jnp.float32)
    kappa = freq * (2.0 * math.pi / size)
    return kappa * kappa


def interp_matrix(size):
    fine_rows = lax.broadcasted_iota(jnp.int32, (2 * size, size), 0)
    coarse_cols = lax.broadcasted_iota(jnp.int32, (2 * size, size), 1)
    base = fine_rows // 2
    odd = fine_rows % 2
    take_base = jnp.where(coarse_cols == base, jnp.where(odd == 0, 1.0, 0.5), 0.0)
    take_next = jnp.where((odd == 1) & (coarse_cols == (base + 1) % size), 0.5, 0.0)
    return (take_base + take_next).astype(jnp.float32)


def spectral_solve(rhs, basis_x, basis_y, basis_z, factor):
    planes, size_y, size_z = rhs.shape
    flat = jnp.dot(rhs.reshape(planes * size_y, size_z), basis_z.T, precision=HIGHEST)
    field = flat.reshape(planes, size_y, size_z)
    field = jnp.einsum("ky,xyz->kxz", basis_y, field, precision=HIGHEST)
    field = lax.all_to_all(field, "space", split_axis=0, concat_axis=1, tiled=True)
    field = jnp.einsum("kx,yxz->kyz", basis_x, field, precision=HIGHEST) * factor
    field = jnp.einsum("kx,kyz->xyz", basis_x, field, precision=HIGHEST)
    field = lax.all_to_all(field, "space", split_axis=0, concat_axis=1, tiled=True)
    field = jnp.matmul(basis_y.T, field, precision=HIGHEST)
    flat = jnp.dot(field.reshape(planes * size_y, size_z), basis_z, precision=HIGHEST)
    return flat.reshape(planes, size_y, size_z)


def pool_matrix(size):
    rows = lax.broadcasted_iota(jnp.int32, (size // 2, size), 0)
    cells = lax.broadcasted_iota(jnp.int32, (size // 2, size), 1)
    return jnp.where(cells // 2 == rows, 0.5, 0.0).astype(jnp.float32)


def restrict(stacked):
    k, a, b, c = stacked.shape
    planes = stacked.reshape(k, a // 2, 2, b, c)
    planes = 0.5 * (planes[:, :, 0] + planes[:, :, 1])
    half = jnp.einsum("kayz,cz->kayc", planes, pool_matrix(c), precision=HIGHEST)
    return jnp.matmul(pool_matrix(b), half, precision=HIGHEST)


def coarse_rate(stacked):
    padded = extended(stacked, (("space", 1),), 1)
    lap = padded[:, 2:] + padded[:, :-2]
    lap = lap + jnp.roll(stacked, -1, 2) + jnp.roll(stacked, 1, 2)
    lap = lap + jnp.roll(stacked, -1, 3) + jnp.roll(stacked, 1, 3)
    return EPS2 * ((lap - 6.0 * stacked) * 0.25) + react(stacked)


def spread(values, following, axis):
    middle = 0.5 * (values + following)
    both = jnp.stack([values, middle], axis=axis + 1)
    shape = list(values.shape)
    shape[axis] = shape[axis] * 2
    return both.reshape(shape)


def refine(stacked, upper):
    matrix_y = interp_matrix(stacked.shape[2])
    matrix_z = interp_matrix(stacked.shape[3])
    both = jnp.concatenate([stacked, upper], axis=1)
    both = jnp.einsum("kayc,zc->kayz", both, matrix_z, precision=HIGHEST)
    both = jnp.matmul(matrix_y, both, precision=HIGHEST)
    planes = stacked.shape[1]
    return spread(both[:, :planes], both[:, 1:], 1)


def coarse_sweep(start, rates, sums):
    first = start + 0.25 * (coarse_rate(start[None])[0] - rates[0]) + sums[0]
    second = first + 0.25 * (coarse_rate(first[None])[0] - rates[1]) + sums[1]
    return (first, second)


def on_device(fine_nodes, fine_implicit):
    nodes = fine_nodes[0]
    implicit = fine_implicit[0]
    planes, size_y, size_z = (nodes.shape[1], nodes.shape[2], nodes.shape[3])
    devices = lax.axis_size("space")
    size_x = planes * devices
    local_y = size_y // devices
    basis_x = real_basis(size_x)
    basis_y = real_basis(size_y)
    basis_z = real_basis(size_z)
    columns = lax.axis_index("space") * local_y + lax.iota(jnp.int32, local_y)
    lam = wave_square(lax.iota(jnp.int32, size_x), size_x)[:, None, None]
    lam = lam + wave_square(columns, size_y)[None, :, None]
    lam = lam + wave_square(lax.iota(jnp.int32, size_z), size_z)[None, None, :]
    factor = 1.0 / (1.0 + 0.5 * lam)
    explicit_old = react(nodes)
    rates_old = explicit_old + implicit
    values = [nodes[0]]
    terms = [implicit[0]]
    for m in range(2):
        w = WEIGHTS[m]
        quad = 0.5 * (w[0] * rates_old[0] + w[1] * rates_old[1] + w[2] * rates_old[2])
        rhs = (
            values[m] + 0.25 * (react(values[m]) - explicit_old[m]) - 0.25 * implicit[m + 1] + quad
        )
        solved = spectral_solve(rhs, basis_x, basis_y, basis_z, factor)
        values.append(solved)
        terms.append((solved - rhs) * 4.0)
    carried = passed_along(values[2], "tm", 1)
    fresh = jnp.stack(values)
    rates_new = react(fresh) + jnp.stack(terms)
    sums = restrict(
        jnp.stack(
            [
                0.5 * (w[0] * rates_new[0] + w[1] * rates_new[1] + w[2] * rates_new[2])
                for w in WEIGHTS
            ]
        )
    )
    coarse = restrict(fresh)
    rates_c = coarse_rate(coarse[:2])
    slot = lax.axis_index("tm")
    slices = lax.axis_size("tm")
    start = coarse[0]
    for section in range(slices - 1):
        first, second = coarse_sweep(start, rates_c, sums)
        received = passed_along(second, "tm", 1)
        start = jnp.where(slot == 0, coarse[0], received)
    first, second = coarse_sweep(start, rates_c, sums)
    delta = jnp.stack([first - coarse[1], second - coarse[2]])
    upper = shifted(delta[:, :1], "space", -1)
    corr = refine(delta, upper)
    fixed_one = values[1] + corr[0]
    fixed_two = values[2] + corr[1]
    late_delta, late_upper = passed_along((delta[1:], upper[1:]), "tm", 1)
    received_end = carried + refine(late_delta, late_upper)[0]
    head = jnp.where(slot == 0, nodes[0], received_end)
    return (jnp.stack([head, fixed_one, fixed_two])[None], jnp.stack([terms[1], terms[2]])[None])


BF16 = jnp.bfloat16
F32 = jnp.float32
MESH = pl.DeviceIdType.MESH
CHUNKS = 2
LANES = 128
GROUP = 8
V0, V1, V2, S0, S1 = range(5)


def host_basis(size):
    rows = np.arange(size)[:, None]
    cells = np.arange(size)[None, :]
    half = size // 2
    freq = np.where(rows <= half, rows, rows - half)
    phase = (freq * cells % size) * (2.0 * math.pi / size)
    scale = np.where((rows == 0) | (rows == half), 1.0 / math.sqrt(size), math.sqrt(2.0 / size))
    return np.where(rows <= half, np.cos(phase), np.sin(phase)) * scale


def two_parts(matrix):
    high = matrix.astype(np.float32).astype(ml_dtypes.bfloat16)
    low = (matrix - high.astype(np.float64)).astype(np.float32).astype(ml_dtypes.bfloat16)
    return jnp.asarray(np.stack([high, low]))


def split(value):
    high = value.astype(BF16)
    return high, (value - high.astype(F32)).astype(BF16)


def product(a, b):
    return jnp.dot(a, b, preferred_element_type=F32)


def left(matrix, value):
    high, low = split(value)
    return product(matrix[0], high) + (product(matrix[0], low) + product(matrix[1], high))


def right(value, matrix):
    high, low = split(value)
    return product(high, matrix[0]) + (product(low, matrix[0]) + product(high, matrix[1]))


def right_exact(value, matrix):
    high, low = split(value)
    return product(high, matrix[...]) + product(low, matrix[...])


def rate(value):
    size_y, size_z = value.shape[1:]
    mid = value[1:-1]
    lap = value[2:] + value[:-2]
    lap = lap + pltpu.roll(mid, 1, 1) + pltpu.roll(mid, size_y - 1, 1)
    lap = lap + pltpu.roll(mid, 1, 2) + pltpu.roll(mid, size_z - 1, 2)
    return EPS2 * ((lap - 6.0 * mid) * 0.25) + react(mid)


def kernel(
    nodes, implicit, bz, bzt, bx, bxt, by, byt, pz, iz,
    out_n, out_i,
    send_a, recv_a, send_b, recv_b, passed, factor, pool, ext, va, vb, delta, rows, grid, early,
    a2a_send, a2a_recv, halo_send, halo_recv, time_send, time_recv, piece_send, piece_recv,
):
    slot = lax.axis_index("tm")
    me = lax.axis_index("space")
    devices = lax.axis_size("space")
    planes, size_y, size_z = nodes.shape[2:]
    size_x = planes * devices
    block = planes * GROUP

    barrier = pltpu.get_barrier_semaphore()

    def greet(k, carry):
        pl.semaphore_signal(
            barrier, inc=1, device_id=(slot, lax.rem(me + k, devices)), device_id_type=MESH
        )
        return carry

    lax.fori_loop(1, devices, greet, 0)
    pl.semaphore_signal(barrier, inc=1, device_id=(1 - slot, me), device_id_type=MESH)

    def part(index):
        return pl.ds(pl.multiple_of(index * block, block), block)

    def exchange(src, dst, m, c, phase, k):
        target = lax.rem(me + k, devices)
        return pltpu.make_async_remote_copy(
            src_ref=src.at[m, c, part(target)],
            dst_ref=dst.at[m, c, part(me)],
            send_sem=a2a_send.at[phase, c, k],
            recv_sem=a2a_recv.at[phase, c, k],
            device_id=(slot, target),
            device_id_type=MESH,
        )

    def start_all(src, dst, m, c, phase):
        def body(k, carry):
            exchange(src, dst, m, c, phase, k).start()
            return carry

        lax.fori_loop(1, devices, body, 0)
        dst[m, c, part(me), :] = src[m, c, part(me), :]

    def wait_all(src, dst, m, c, phase):
        def body(k, carry):
            exchange(src, dst, m, c, phase, k).wait_recv()
            return carry

        lax.fori_loop(1, devices, body, 0)

    def beside(first, count, low, size, put, step, index):
        return pltpu.make_async_remote_copy(
            src_ref=ext.at[pl.ds(first, count), pl.ds(low, size)],
            dst_ref=ext.at[pl.ds(first, count), pl.ds(put, size)],
            send_sem=halo_send.at[index],
            recv_sem=halo_recv.at[index],
            device_id=(slot, lax.rem(me + step, devices)),
            device_id_type=MESH,
        )

    halos = [
        beside(V0, 1, 5, 3, 1, 1, 0),
        beside(V0, 1, 4, 4, 8, devices - 1, 1),
        beside(V1, 1, 5, 3, 1, 1, 2),
        beside(V1, 1, 4, 4, 8, devices - 1, 3),
        beside(S0, 2, 5, 3, 1, 1, 4),
        beside(S0, 2, 4, 4, 8, devices - 1, 5),
        beside(V2, 1, 4, 1, 8, devices - 1, 6),
    ]

    def ahead(src, dst, index):
        return pltpu.make_async_remote_copy(
            src_ref=src,
            dst_ref=dst,
            send_sem=time_send.at[index],
            recv_sem=time_recv.at[index],
            device_id=(1 - slot, me),
            device_id_type=MESH,
        )

    handed = [
        ahead(vb.at[pl.ds(2, 9)], va.at[pl.ds(2, 9)], 0),
        ahead(delta.at[1], delta.at[2], 1),
    ]

    def piece(c, k):
        source = lax.rem(me + devices - k, devices)
        return pltpu.make_async_remote_copy(
            src_ref=recv_b.at[1, c, part(source)],
            dst_ref=passed.at[c, part(source)],
            send_sem=piece_send.at[c, k],
            recv_sem=piece_recv.at[c, k],
            device_id=(1 - slot, me),
            device_id_type=MESH,
        )

    def quad(m, terms):
        w = WEIGHTS[m]
        return 0.5 * (w[0] * terms[0] + w[1] * terms[1] + w[2] * terms[2])

    def old_rates(x):
        return [react(nodes[0, j, x]) + implicit[0, j, x] for j in range(3)]

    def forward(rhs, x, m):
        field = left(by, right(rhs, bzt))
        for c in range(CHUNKS):
            for d in range(size_y // GROUP):
                send_a[m, c, pl.ds(pl.multiple_of(d * block + x * GROUP, GROUP), GROUP), :] = field[
                    d * GROUP : (d + 1) * GROUP, c * LANES : (c + 1) * LANES
                ]

    def undo(chunk, c, x):
        return left(
            byt,
            jnp.concatenate(
                [
                    chunk(c, pl.ds(pl.multiple_of(d * block + x * GROUP, GROUP), GROUP))
                    for d in range(size_y // GROUP)
                ],
                axis=0,
            ),
        )

    def prepare(chunk):
        def body(x, carry):
            early[x] = undo(chunk, 0, x)
            return carry

        lax.fori_loop(0, planes, body, 0, unroll=4)

    def backward(chunk, x):
        return right(jnp.concatenate([early[x], undo(chunk, 1, x)], axis=1), bz)

    def first_rhs(x, carry):
        rhs = nodes[0, 0, x] - 0.25 * implicit[0, 1, x] + quad(0, old_rates(x))
        out_i[0, 0, x] = rhs
        forward(rhs, x, 0)
        return carry

    lax.fori_loop(0, planes, first_rhs, 0, unroll=8)
    pl.semaphore_wait(barrier, devices)

    def waves(index, size):
        half = size // 2
        freq = jnp.where(index <= half, index, index - half).astype(F32)
        kappa = freq * (2.0 * math.pi / size)
        return kappa * kappa

    def solve_lines(m, c):
        lines = jnp.concatenate(
            [recv_a[m, c, pl.ds(k, size_x, stride=GROUP), :] for k in range(GROUP)], axis=1
        )
        field = left(bxt, left(bx, lines) * factor[c])
        for k in range(GROUP):
            send_b[m, c, pl.ds(k, size_x, stride=GROUP), :] = field[:, k * LANES : (k + 1) * LANES]

    def average(index, value):
        pool[index] = right_exact(value, pz)
        return 0.5 * (
            pool[index, pl.ds(0, size_y // 2, stride=2), :]
            + pool[index, pl.ds(1, size_y // 2, stride=2), :]
        )

    for c in range(CHUNKS):
        start_all(send_a, recv_a, 0, c, 0)

    shape = (size_x, LANES)
    lam_x = waves(lax.broadcasted_iota(jnp.int32, shape, 0), size_x)
    for c in range(CHUNKS):
        lam_z = waves(lax.broadcasted_iota(jnp.int32, shape, 1) + c * LANES, size_z)
        for k in range(GROUP):
            lam_y = waves(jnp.full(shape, me * GROUP + k, jnp.int32), size_y)
            factor[c, :, k * LANES : (k + 1) * LANES] = 1.0 / (1.0 + 0.5 * (lam_x + lam_y + lam_z))

    def pool_start(p, carry):
        ext[V0, 4 + p] = average(0, 0.5 * (nodes[0, 0, 2 * p] + nodes[0, 0, 2 * p + 1]))
        return carry

    lax.fori_loop(0, planes // 2, pool_start, 0)
    halos[0].start()
    halos[1].start()

    def transfer_lines(m):
        for c in range(CHUNKS):
            wait_all(send_a, recv_a, m, c, 2 * m)
            solve_lines(m, c)
            start_all(send_b, recv_b, m, c, 2 * m + 1)

    transfer_lines(0)
    for c in range(CHUNKS):
        wait_all(send_b, recv_b, 0, c, 1)
        if c == 0:
            prepare(lambda c, at: recv_b[0, c, at, :])

    def middle(x, carry):
        solved = backward(lambda c, at: recv_b[0, c, at, :], x)
        term = (solved - out_i[0, 0, x]) * 4.0
        out_n[0, 1, x] = solved
        out_i[0, 0, x] = term
        rhs = (
            solved
            + 0.25 * (react(solved) - react(nodes[0, 1, x]))
            - 0.25 * implicit[0, 2, x]
            + quad(1, old_rates(x))
        )
        out_i[0, 1, x] = rhs
        forward(rhs, x, 1)
        return carry

    lax.fori_loop(0, planes, middle, 0, unroll=8)
    for c in range(CHUNKS):
        start_all(send_a, recv_a, 1, c, 2)

    def pool_middle(p, carry):
        ext[V1, 4 + p] = average(0, 0.5 * (out_n[0, 1, 2 * p] + out_n[0, 1, 2 * p + 1]))
        return carry

    lax.fori_loop(0, planes // 2, pool_middle, 0)
    halos[2].start()
    halos[3].start()

    transfer_lines(1)
    for c in range(CHUNKS):
        @pl.when(slot == 0)
        def _():
            piece(c, 0).start()

        def arrive(k, carry):
            exchange(send_b, recv_b, 1, c, 3, k).wait_recv()

            @pl.when(slot == 0)
            def _():
                piece(c, k).start()

            return carry

        lax.fori_loop(1, devices, arrive, 0)

        if c == 0:
            prepare(lambda c, at: recv_b[1, c, at, :])

    def last(p, carry):
        quads = [0.0, 0.0]
        total = 0.0
        for x in (2 * p, 2 * p + 1):
            solved = backward(lambda c, at: recv_b[1, c, at, :], x)
            term = (solved - out_i[0, 1, x]) * 4.0
            out_n[0, 2, x] = solved
            out_i[0, 1, x] = term
            fresh = [
                react(nodes[0, 0, x]) + implicit[0, 0, x],
                react(out_n[0, 1, x]) + out_i[0, 0, x],
                react(solved) + term,
            ]
            quads = [quads[m] + quad(m, fresh) for m in range(2)]
            total = total + solved
        ext[S0, 4 + p] = average(0, 0.5 * quads[0])
        ext[S1, 4 + p] = average(1, 0.5 * quads[1])
        ext[V2, 4 + p] = average(2, 0.5 * total)
        return carry

    lax.fori_loop(0, planes // 2, last, 0, unroll=4)
    for halo in halos[4:]:
        halo.start()
    for halo in halos:
        halo.wait_recv()

    @pl.when(slot == 0)
    def _():
        first = ext[V0, 1:12] + ext[S0, 1:12]
        second = first[1:-1] + 0.25 * (rate(first) - rate(ext[V1, 1:12])) + ext[S1, 2:11]
        vb[2:11] = second
        handed[0].start()
        delta[0] = first[3:8] - ext[V1, 4:9]
        delta[1] = second[2:7] - ext[V2, 4:9]
        handed[1].start()

    @pl.when(slot == 1)
    def _():
        handed[0].wait_recv()
        begin = va[2:11]
        first = begin[1:-1] + 0.25 * (rate(begin) - rate(ext[V0, 2:11])) + ext[S0, 3:10]
        second = first[1:-1] + 0.25 * (rate(first) - rate(ext[V1, 3:10])) + ext[S1, 4:9]
        delta[0] = first[1:6] - ext[V1, 4:9]
        delta[1] = second - ext[V2, 4:9]

    def refined(index):
        def body(p, carry):
            coarse = delta[index, p]
            rows[p, pl.ds(0, size_y // 2, stride=2), :] = coarse
            rows[p, pl.ds(1, size_y // 2, stride=2), :] = 0.5 * (
                coarse + pltpu.roll(coarse, size_y // 2 - 1, 0)
            )
            grid[p] = right_exact(rows[p], iz)
            return carry

        lax.fori_loop(0, planes // 2 + 1, body, 0, unroll=True)

    def correct(index, base, target):
        refined(index)

        def body(p, carry):
            out_n[0, target, 2 * p] = base(2 * p) + grid[p]
            out_n[0, target, 2 * p + 1] = base(2 * p + 1) + 0.5 * (grid[p] + grid[p + 1])
            return carry

        lax.fori_loop(0, planes // 2, body, 0, unroll=2)

    correct(0, lambda x: out_n[0, 1, x], 1)
    correct(1, lambda x: out_n[0, 2, x], 2)

    @pl.when(slot == 0)
    def _():
        out_n[0, 0] = nodes[0, 0]
        for copy in handed:
            copy.wait_send()
        for c in range(CHUNKS):

            def left_here(k, carry, c=c):
                piece(c, k).wait_send()
                return carry

            lax.fori_loop(0, devices, left_here, 0)

    @pl.when(slot == 1)
    def _():
        for c in range(CHUNKS):

            def landed(k, carry, c=c):
                piece(c, k).wait_recv()
                return carry

            lax.fori_loop(0, devices, landed, 0)
            if c == 0:
                prepare(lambda c, at: passed[c, at, :])

        handed[1].wait_recv()
        correct(2, lambda x: backward(lambda c, at: passed[c, at, :], x), 0)

    for phase, (src, dst) in enumerate([(send_a, recv_a), (send_b, recv_b)] * 2):
        for c in range(CHUNKS):

            def body(k, carry, src=src, dst=dst, phase=phase, c=c):
                exchange(src, dst, phase // 2, c, phase, k).wait_send()
                return carry

            lax.fori_loop(1, devices, body, 0)
    for halo in halos:
        halo.wait_send()


def fused(fine_nodes, fine_implicit):
    planes, size_y, size_z = fine_nodes.shape[2:]
    devices = lax.axis_size("space")
    basis_x = host_basis(planes * devices)
    basis_y = host_basis(size_y)
    basis_z = host_basis(size_z)
    cells = np.arange(size_z)
    half = np.zeros((size_z, size_z // 2))
    half[cells, cells // 2] = 0.5
    lines = np.zeros((size_z // 2, size_z))
    coarse = np.arange(size_z // 2)
    lines[coarse, 2 * coarse] = 1.0
    lines[coarse, 2 * coarse + 1] += 0.5
    lines[(coarse + 1) % (size_z // 2), 2 * coarse + 1] += 0.5
    constants = [
        two_parts(m) for m in (basis_z, basis_z.T, basis_x, basis_x.T, basis_y, basis_y.T)
    ]
    constants.append(jnp.asarray(half.astype(ml_dtypes.bfloat16)))
    constants.append(jnp.asarray(lines.astype(ml_dtypes.bfloat16)))
    field = (2, CHUNKS, devices * planes * GROUP, LANES)
    plane = (size_y // 2, size_z // 2)
    vmem = pl.BlockSpec(memory_space=pltpu.VMEM)
    shape_n = fine_nodes.shape
    shape_i = shape_n[:1] + (2,) + shape_n[2:]
    return pl.pallas_call(
        kernel,
        out_shape=(jax.ShapeDtypeStruct(shape_n, F32), jax.ShapeDtypeStruct(shape_i, F32)),
        in_specs=[vmem] * 10,
        out_specs=(vmem, vmem),
        scratch_shapes=[
            pltpu.VMEM(field, F32),
            pltpu.VMEM(field, F32),
            pltpu.VMEM(field, F32),
            pltpu.VMEM(field, F32),
            pltpu.VMEM(field[1:], F32),
            pltpu.VMEM((CHUNKS, planes * devices, GROUP * LANES), F32),
            pltpu.VMEM((3, size_y, size_z // 2), F32),
            pltpu.VMEM((5, 12) + plane, F32),
            pltpu.VMEM((12,) + plane, F32),
            pltpu.VMEM((12,) + plane, F32),
            pltpu.VMEM((3, 5) + plane, F32),
            pltpu.VMEM((5, size_y, size_z // 2), F32),
            pltpu.VMEM((5, size_y, size_z), F32),
            pltpu.VMEM((planes, size_y, LANES), F32),
            pltpu.SemaphoreType.DMA((4, CHUNKS, devices)),
            pltpu.SemaphoreType.DMA((4, CHUNKS, devices)),
            pltpu.SemaphoreType.DMA((7,)),
            pltpu.SemaphoreType.DMA((7,)),
            pltpu.SemaphoreType.DMA((2,)),
            pltpu.SemaphoreType.DMA((2,)),
            pltpu.SemaphoreType.DMA((CHUNKS, devices)),
            pltpu.SemaphoreType.DMA((CHUNKS, devices)),
        ],
        compiler_params=pltpu.CompilerParams(
            collective_id=0, has_side_effects=True, vmem_limit_bytes=56 * 2**20
        ),
    )(fine_nodes, fine_implicit, *constants)


def either(fine_nodes, fine_implicit):
    planes, size_y, size_z = fine_nodes.shape[2:]
    devices = lax.axis_size("space")
    fits = planes == GROUP and size_y == GROUP * devices and size_z == CHUNKS * LANES
    if fits and lax.axis_size("tm") == 2:
        return fused(fine_nodes, fine_implicit)
    return on_device(fine_nodes, fine_implicit)


def solution(mesh):
    return jax.shard_map(
        either,
        mesh=mesh,
        in_specs=(P("tm", None, "space", None, None), P("tm", None, "space", None, None)),
        out_specs=(P("tm", None, "space", None, None), P("tm", None, "space", None, None)),
        check_vma=False,
    )
```
